1024 devices in a mesh: dp: 16 (over y_lo, z), expert: 64 (over x, y_hi, core).
Axes of the slice: x: 8, y: 8 (y_hi: 4, y_lo: 2; y = y_hi * 2 + y_lo), z: 8, core: 2. Of those that a mesh axis runs over, the one named last changes fastest.
Arguments:
- out_grad: bfloat16 [3072, 7168], P('expert', 'dp'), may hold values from -6 to 6
- gate_weight: float32 [3072, 8], P('expert'), may hold values from 0.05 to 0.5
- expert_ids: int32 [3072, 8], P('expert'), may hold values from 0 to 63, all different within a row; in each aligned block of 48 rows (0 to 47, 48 to 95, ...) at most 9 rows name the same one
- replicated: int32 [64], replicated, may hold values from 0 to 1, as said below
- down_weight: bfloat16 [64, 1024, 7168], P('expert', None, 'dp'), may hold values from -0.0625 to 0.0625
- pre_act: bfloat16 [64, 2, 576, 2048], P('expert', None, 'dp'), may hold values from -6 to 6
Outputs:
- grad_down: bfloat16 [64, 1024, 7168], P('expert', None, 'dp')
- grad_pre: bfloat16 [64, 2, 576, 2048], P('expert', None, 'dp')
The draws below stay inside these ranges and needn't reach their ends.
Inputs may be any that keep to these rules, and one draw needn't show every extreme that they name: `expert_ids`: each row names 8 different experts; among the 48 rows of one device no expert is named more than 9 times, a bound that some block reaches. `replicated`: expert 0 always has a redundant slot; each other expert has one with chance one half.
All inputs are finite; a program needn't handle non-finite values.
Results may differ from the reference program's by a relative error of at most 0.018.
Values may be sent and summed in bfloat16 or wider, within the bound.
A program may use at most 32 MiB of HBM per device.

```python
import math
import jax
import jax.numpy as jnp
import numpy as np
from jax import lax

D = 7168
TOPK = 8
F = 1024
TOK_DEV = 48
TOKENS = 3072
CAP = 9
ROWS = 576
N_DP = 16
N_EXPERT = 64


def draw_replicated(key, part):
    flags = jax.random.randint(jax.random.fold_in(key, 7), (N_EXPERT,), 0, 2).astype(jnp.int32)
    return flags.at[0].set(1)


def block_levels(key, extent, shards, smallest, top_value):
    def one(axis_at, parts):
        heights = jax.random.uniform(jax.random.fold_in(jax.random.fold_in(key, 6), axis_at), (parts,), jnp.float32, smallest / len(shards), top_value / len(shards))
        return jnp.repeat(jnp.exp(heights), extent[axis_at] // parts).reshape((-1,) + (1,) * (len(extent) - axis_at - 1))

    gain = one(*shards[0])
    for cut in shards[1:]:
        gain = gain * one(*cut)
    return gain


def assign_block(rng, own, number, rows, number_of, top, most, skew):
    ranking = jax.random.permutation(rng, number_of)
    packed, common = shares(number_of, rows * top, most, skew, True), shares(number_of, rows * top, most, skew, False)
    places = jnp.arange(number_of)

    def named(lengths, rotation):
        used = int((lengths > 0).sum())
        fixed = max(1, used // 4)
        moved = fixed + (places - fixed + rotation * (used - fixed)) % max(1, number_of - fixed)
        return jnp.zeros((number_of,), jnp.int32).at[ranking[jnp.where(places < fixed, places, moved)]].set(jnp.asarray(lengths, jnp.int32))

    lengths = jnp.where(number % 4 == 0, named(packed, number // 4), named(common, number - number // 4 - 1))
    mixed = jax.random.permutation(jax.random.fold_in(own, 3), number_of)
    giver, sink = mixed[0:number_of // 2 * 2:2], mixed[1:number_of // 2 * 2:2]
    margin = jnp.minimum(lengths[giver] - 1, most - lengths[sink]) // 2
    margin = jnp.where((giver == ranking[0]) | (sink == ranking[0]) | (lengths[sink] == 0), 0, jnp.maximum(margin, 0))
    moved = jax.random.randint(jax.random.fold_in(own, 4), (number_of // 2,), 0, 1 << 20) % (margin + 1)
    lengths = lengths.at[giver].add(-moved).at[sink].add(moved)
    items = jnp.searchsorted(jnp.cumsum(lengths), jnp.arange(rows * top), side="right").astype(jnp.int32)
    grid = items.reshape(top, rows).T
    grid = grid[jax.random.permutation(jax.random.fold_in(own, 1), rows)]
    rotation = jax.random.randint(jax.random.fold_in(own, 2), (rows, 1), 0, top)
    return jnp.take_along_axis(grid, (jnp.arange(top)[None, :] + rotation) % top, axis=1)


def shares(count, total, bound, skew, full):
    loads = [(1 << 20) // math.isqrt(grade ** skew) + 1 for grade in range(1, count + 1)]
    largest = bound if full else min(bound, max(-(-total // count), total * loads[0] // sum(loads)))
    least = 1 if total - largest >= count - 1 else 0
    given, rest = [largest] + [least] * (count - 1), total - largest - least * (count - 1)
    while rest > 0:
        free = [i for i in range(1, count) if given[i] < largest] or [i for i in range(1, count) if given[i] < bound]
        whole, remaining = sum([loads[i] for i in free]), rest
        for i in free:
            extra = min(bound - given[i], max(1, remaining * loads[i] // whole), rest)
            given[i] = given[i] + extra
            rest = rest - extra
    return np.array(given)


def bell_draw(key, shape, spread, most, shards=(), held_as=jnp.bfloat16):
    gain = block_levels(key, shape, shards, -0.22, 0.18) if shards else 1.0
    result = jax.random.normal(key, shape, jnp.float32) * spread * gain
    return jnp.minimum(jnp.maximum(result, -most), most).astype(held_as)


def setup_inputs(seed: int = 0) -> dict:
    key_of = jax.random.split(jax.random.key(seed), 7)
    out_grad = bell_draw(key_of[0], (TOKENS, D), 1.0, 6.0, ((0, 64), (1, 16)))
    gate_weight = jnp.clip(jnp.exp(math.log(0.5) - 2.3025851 * jax.random.uniform(key_of[1], (TOKENS, TOPK), jnp.float32) ** block_levels(key_of[1], (TOKENS, TOPK), ((0, 64),), -0.2, 0.2)), 0.05, 0.5)
    expert_ids_keys = jax.random.split(jax.random.fold_in(key_of[2], 1), TOKENS // TOK_DEV)
    expert_ids_turns = jax.random.permutation(jax.random.fold_in(key_of[2], 3), TOKENS // TOK_DEV)
    expert_ids = jax.vmap(lambda own, number: assign_block(jax.random.fold_in(key_of[2], 2), own, number, TOK_DEV, N_EXPERT, TOPK, CAP, 1))(expert_ids_keys, expert_ids_turns).reshape((TOKENS, TOPK))
    replicated = draw_replicated(jax.random.fold_in(key_of[6], 71), 0)
    down_weight = bell_draw(key_of[4], (N_EXPERT, F, D), D ** -0.5, 0.0625, ((0, 64), (2, 16)))
    pre_act = bell_draw(key_of[5], (N_EXPERT, 2, ROWS, 2 * F), 1.0, 6.0, ((0, 64), (2, 16)))
    return dict(out_grad=out_grad, gate_weight=gate_weight, expert_ids=expert_ids, replicated=replicated, down_weight=down_weight, pre_act=pre_act)


def hidden_of(stored):
    width = stored.shape[-1] // 2
    gate_part = stored[..., :width].astype(jnp.float32)
    up_part = stored[..., width:].astype(jnp.float32)
    return (gate_part * jax.nn.sigmoid(gate_part) * up_part).astype(jnp.bfloat16)


def swiglu_back(hidden_grad, stored):
    width = stored.shape[-1] // 2
    gate_part = stored[..., :width].astype(jnp.float32)
    up_part = stored[..., width:].astype(jnp.float32)
    sigmoid_v = jax.nn.sigmoid(gate_part)
    gate_grad = hidden_grad * up_part * sigmoid_v * (1.0 + gate_part * (1.0 - sigmoid_v))
    up_grad = hidden_grad * gate_part * sigmoid_v
    return jnp.concatenate([gate_grad, up_grad], axis=-1).astype(jnp.bfloat16)


def width_sum(rows, weight):
    block = D // N_DP
    left = rows.astype(jnp.float32).reshape(rows.shape[0], N_DP, block)
    right = weight.astype(jnp.float32).reshape(weight.shape[0], N_DP, block)
    terms = jnp.einsum("rnd,fnd->nrf", left, right, precision=lax.Precision.HIGHEST)
    rounded = lax.optimization_barrier(terms.astype(jnp.bfloat16)).astype(jnp.float32)
    return jnp.sum(rounded, axis=0)


def reference(out_grad, gate_weight, expert_ids, replicated, down_weight, pre_act):
    half_way = N_EXPERT // 2
    route_ids = expert_ids.reshape(N_EXPERT, TOK_DEV * TOPK)
    experts_iota = jnp.arange(N_EXPERT, dtype=jnp.int32)
    onehot = (route_ids[:, :, None] == experts_iota[None, None, :]).astype(jnp.int32)
    position = jnp.sum(onehot * (jnp.cumsum(onehot, axis=1) - 1), axis=2).astype(jnp.int32)
    source = jnp.broadcast_to(experts_iota[:, None], route_ids.shape)
    rep_of = replicated[route_ids]
    diverted = (rep_of == 1) & (source % 2 == 1)
    target_dev = jnp.where(diverted, (route_ids + half_way) % N_EXPERT, route_ids).reshape(-1)
    slot_index = diverted.astype(jnp.int32)
    flat_index = (slot_index * ROWS + source * CAP + position).reshape(-1).astype(jnp.int32)
    scaled = gate_weight.reshape(-1)[:, None] * jnp.repeat(out_grad.astype(jnp.float32), TOPK, axis=0)
    routed = scaled.astype(jnp.bfloat16)

    def dispatch_for(device):
        scatter_index = jnp.where(target_dev == device, flat_index, 2 * ROWS).astype(jnp.int32)
        buffer = jnp.zeros((2 * ROWS, D), routed.dtype).at[scatter_index].set(routed, mode="drop")
        return buffer.reshape(2, ROWS, D)

    def per_expert(expert):
        partner = ((expert + half_way) % N_EXPERT).astype(jnp.int32)
        own_rows = dispatch_for(expert)
        theirs = dispatch_for(partner)[1]
        own_weight = down_weight[expert]
        rep_weight = down_weight[partner]
        grad_own = width_sum(own_rows[0], own_weight)
        grad_rep = width_sum(own_rows[1], rep_weight)
        stored = pre_act[expert]
        pre_own = swiglu_back(grad_own, stored[0])
        pre_rep = swiglu_back(grad_rep, stored[1])
        hidden_own = hidden_of(stored[0])
        hidden_rep = hidden_of(pre_act[partner, 1])
        weight_grad = jnp.dot(hidden_own.T, own_rows[0], preferred_element_type=jnp.float32)
        weight_grad = weight_grad + jnp.dot(hidden_rep.T, theirs, preferred_element_type=jnp.float32)
        return weight_grad.astype(jnp.bfloat16), jnp.stack([pre_own, pre_rep])

    grad_down, grad_pre = lax.map(per_expert, experts_iota)
    return grad_down, grad_pre
```

```python
import jax
import jax.numpy as jnp
from jax import lax
from jax.sharding import PartitionSpec as P


def passed_along(value, axis, steps):
    count = lax.axis_size(axis)
    pairs = [(source, (source + steps) % count) for source in range(count)]
    return lax.ppermute(value, axis, pairs)


def hidden_of(stored):
    width = stored.shape[-1] // 2
    gate_part = stored[..., :width].astype(jnp.float32)
    up_part = stored[..., width:].astype(jnp.float32)
    return (gate_part * jax.nn.sigmoid(gate_part) * up_part).astype(jnp.bfloat16)


def swiglu_back(hidden_grad, stored):
    width = stored.shape[-1] // 2
    gate_part = stored[..., :width].astype(jnp.float32)
    up_part = stored[..., width:].astype(jnp.float32)
    sigmoid_v = jax.nn.sigmoid(gate_part)
    gate_grad = hidden_grad * up_part * sigmoid_v * (1.0 + gate_part * (1.0 - sigmoid_v))
    up_grad = hidden_grad * gate_part * sigmoid_v
    return jnp.concatenate([gate_grad, up_grad], axis=-1).astype(jnp.bfloat16)


def on_device(out_grad, gate_weight, expert_ids, replicated, down_weight, pre_act):
    devices = lax.axis_size("expert")
    half_way = devices // 2
    myself = lax.axis_index("expert")
    shares = lax.axis_size("dp")
    share = lax.axis_index("dp")
    tokens_here, choose = expert_ids.shape
    rows_share = pre_act.shape[2]
    all_rows = rows_share * shares
    capacity = all_rows // devices
    routes = tokens_here * choose

    source = (share * rows_share + jnp.arange(rows_share)) // capacity
    mine_replicated = replicated[myself] == 1
    moved = ((source % 2 == 1) & mine_replicated)[:, None]

    hidden = hidden_of(pre_act[0])
    theirs = passed_along(hidden[1], "expert", half_way)
    merged = jnp.where(moved, theirs, hidden[0])
    gathered = lax.all_gather(merged, "dp", axis=0, tiled=True)

    flat_ids = expert_ids.reshape(-1)
    onehot = (flat_ids[:, None] == jnp.arange(devices, dtype=jnp.int32)[None, :])
    order = jnp.arange(routes, dtype=jnp.int32)
    earlier = (order[None, :] < order[:, None]).astype(jnp.bfloat16)
    counts = jnp.dot(earlier, onehot.astype(jnp.bfloat16), preferred_element_type=jnp.float32)
    position = jnp.sum(jnp.where(onehot, counts, 0.0), axis=1).astype(jnp.int32)
    target = flat_ids * capacity + position
    placer = (
        jnp.arange(devices * capacity, dtype=jnp.int32)[:, None] == target[None, :]
    ).astype(jnp.bfloat16)
    scaled = gate_weight[:, :, None] * out_grad.astype(jnp.float32)[:, None, :]
    routed = scaled.astype(jnp.bfloat16).reshape(routes, -1)
    outgoing = jnp.dot(placer, routed, preferred_element_type=jnp.float32).astype(jnp.bfloat16)
    outgoing = outgoing.reshape(devices, capacity, -1)
    arrived = lax.all_to_all(outgoing, "expert", split_axis=0, concat_axis=0, tiled=True)
    arrived = arrived.reshape(all_rows, -1)

    partial_value = jnp.einsum(
        "rd,fd->rf", arrived, down_weight[0], preferred_element_type=jnp.float32
    ).astype(jnp.bfloat16)
    parts = lax.all_to_all(
        partial_value.reshape(shares, rows_share, -1), "dp", split_axis=0, concat_axis=0, tiled=True
    )
    summed = jnp.sum(parts.astype(jnp.float32), axis=0)
    elsewhere = passed_along(
        jnp.where(moved, summed, 0.0).astype(jnp.bfloat16), "expert", half_way
    ).astype(jnp.float32)
    slots = jnp.stack([jnp.where(moved, 0.0, summed), elsewhere])
    grad_pre = swiglu_back(slots, pre_act[0])[None]

    grad_down = jnp.einsum(
        "rf,rd->fd", gathered, arrived, preferred_element_type=jnp.float32
    ).astype(jnp.bfloat16)[None]
    return (grad_down, grad_pre)


def solution(mesh):
    in_specs = (
        P("expert", "dp"),
        P("expert", None),
        P("expert", None),
        P(),
        P("expert", None, "dp"),
        P("expert", None, "dp", None),
    )
    out_specs = (P("expert", None, "dp"), P("expert", None, "dp", None))
    return jax.shard_map(
        on_device, mesh=mesh, in_specs=in_specs, out_specs=out_specs, check_vma=False
    )
```

```python
import functools

import jax
import jax.numpy as jnp
import numpy as np
from jax import lax
from jax.experimental import pallas as pl
from jax.experimental.pallas import tpu as pltpu
from jax.sharding import PartitionSpec as P

F32, BF16 = jnp.float32, jnp.bfloat16
CAP = 9
LANES = 128


def up_to(value, step):
    return -(-value // step) * step


class Sizes:
    def __init__(self, mesh):
        self.dp, self.experts = mesh.shape["dp"], mesh.shape["expert"]
        self.nz = self.dp // 2
        self.nx = self.nz
        self.ny = self.experts // (2 * self.nx)
        self.slab = 2 * self.ny
        self.per_share = self.experts // self.dp
        self.share_rows = self.per_share * CAP
        self.half = up_to(self.share_rows, 8)
        self.rows = 2 * self.half


def row_wants(z, tokens):
    wants = np.full((z.rows, z.slab * tokens), -1.0, np.float32)
    for h in range(2):
        for u in range(z.share_rows):
            source = h * z.per_share + u // CAP
            wants[h * z.half + u, source * tokens : (source + 1) * tokens] = u % CAP + 1
    return wants


def stacked(value):
    width = value.shape[1] // 2
    return jnp.concatenate([value[:, :width], value[:, width:]], axis=0)


def kernel(
    z,
    g_ref, hid_ref, moved_ref, wants_ref, wt_ref,
    gd_ref, hg_ref,
    gall, theirs, hbuf, hall, dsend, dbuf, pbuf, prec, ssend, zrec, fsend, frec,
    gy_s, gy_r, gc_s, gc_r, th_s, th_r, hz_s, hz_r, hy_s, hy_r,
    dx_s, dx_r, py_s, py_r, rz_s, rz_r, fx_s, fx_r,
):
    dp, ex = lax.axis_index("dp"), lax.axis_index("expert")
    y_lo, my_z = dp // z.nz, dp % z.nz
    my_x, yc = ex // z.slab, ex % z.slab
    y_hi, core = yc // 2, yc % 2

    def at_z(k):
        return y_lo * z.nz + (my_z + k) % z.nz

    def at_x(k):
        return ((my_x + k) % z.nx) * z.slab + yc

    def in_slab(k):
        return ((y_hi + k) % z.ny) * 2 + core

    def at_y(k):
        return my_x * z.slab + in_slab(k)

    other = (1 - y_lo) * z.nz + my_z
    sibling = my_x * z.slab + y_hi * 2 + 1 - core
    opposite = at_x(z.nx // 2)

    def send(src, dst, s, r, **where):
        copy = pltpu.make_async_remote_copy(
            src_ref=src, dst_ref=dst, send_sem=s, recv_sem=r,
            device_id=where, device_id_type=pl.DeviceIdType.MESH,
        )
        return copy

    barrier = pltpu.get_barrier_semaphore()
    greeted = (
        [dict(dp=at_z(k)) for k in range(1, z.nz)]
        + [dict(dp=other)]
        + [dict(expert=at_x(k)) for k in range(1, z.nx)]
        + [dict(expert=at_y(k)) for k in range(1, z.ny)]
        + [dict(expert=sibling)]
    )
    for where in greeted:
        pl.semaphore_signal(barrier, inc=1, device_id=where, device_id_type=pl.DeviceIdType.MESH)
    pl.semaphore_wait(barrier, len(greeted))

    to_y = [
        send(g_ref, gall.at[yc], gy_s.at[k], gy_r.at[k], expert=at_y(k)) for k in range(1, z.ny)
    ]
    for copy in to_y:
        copy.start()
    to_core = [send(g_ref, gall.at[yc], gc_s.at[0], gc_r.at[0], expert=sibling)]
    to_core[0].start()
    to_partner = send(hid_ref.at[1], theirs, th_s, th_r, expert=opposite)
    to_partner.start()
    gall[yc] = g_ref[...]

    moved = jnp.concatenate([moved_ref[...]] * (hbuf.shape[2] // LANES), axis=1)
    to_partner.wait_recv()
    hbuf[dp] = (
        hid_ref[0].astype(F32) * (1.0 - moved) + theirs[...].astype(F32) * moved
    ).astype(BF16)
    to_z = [
        send(hbuf.at[dp], hbuf.at[dp], hz_s.at[k], hz_r.at[k], dp=at_z(k)) for k in range(1, z.nz)
    ]
    for copy in to_z:
        copy.start()
    to_other = [send(hbuf.at[dp], hbuf.at[dp], hy_s.at[0], hy_r.at[0], dp=other)]
    to_other[0].start()

    for k in range(1, z.ny):
        to_y[k - 1].wait_recv()
        slot = in_slab(z.ny - k)
        copy = send(gall.at[slot], gall.at[slot], gc_s.at[k], gc_r.at[k], expert=sibling)
        copy.start()
        to_core.append(copy)
    for copy in to_core:
        copy.wait_recv()

    tokens = g_ref.shape[0]
    width = wt_ref.shape[0]
    data = gall[...].reshape(z.slab * tokens, g_ref.shape[1])
    table = up_to(width + z.experts, LANES)
    first = table - LANES
    places = data[:, first:table]
    lane = lax.broadcasted_iota(jnp.int32, (z.rows, LANES), 1)
    wants = wants_ref[...]
    to_x = []
    for k in list(range(z.nx // 2, 0, -1)) + [0]:
        for step in (k,) if k in (0, z.nx // 2) else (k, z.nx - k):
            expert = at_x(step)
            chosen = jnp.where(lane == width - first + expert, 1.0, 0.0).astype(BF16)
            ranks = lax.dot_general(
                chosen, places, (((1,), (1,)), ((), ())), preferred_element_type=F32
            )
            picker = jnp.where(ranks == wants, 1.0, 0.0).astype(BF16)
            picked = jnp.dot(picker, data, preferred_element_type=F32)
            about = picked[:, table : table + LANES]
            named = jnp.where((lane < 8) & (about == expert.astype(F32)), 1.0, 0.0)
            parts = sum(pltpu.roll(named, 8 * n, 1) for n in (1, 2, 3))
            weight = jnp.sum(about * parts, axis=1, keepdims=True)
            rows = (picked[:, :table] * weight).astype(BF16)
            if step == 0:
                dbuf[my_x] = rows
            else:
                dsend[step] = rows
                copy = send(
                    dsend.at[step], dbuf.at[my_x], dx_s.at[step], dx_r.at[step], expert=expert
                )
                copy.start()
                to_x.append(copy)

    for k in range(1, z.nz):
        to_z[k - 1].wait_recv()
        slot = at_z(z.nz - k)
        copy = send(hbuf.at[slot], hbuf.at[slot], hy_s.at[k], hy_r.at[k], dp=other)
        copy.start()
        to_other.append(copy)

    per_half = z.nx // 2
    for k in range(0, z.nx // 2 + 1):
        for step in (k,) if k in (0, z.nx // 2) else (z.nx - k, k):
            slab = (my_x + step) % z.nx
            if step:
                back = z.nx - step
                send(
                    dsend.at[back], dbuf.at[slab], dx_s.at[back], dx_r.at[back], expert=at_x(back)
                ).wait_recv()
            part = jnp.dot(dbuf[slab][:, :width], wt_ref[...], preferred_element_type=F32)
            for h in range(2):
                pbuf[slab, h] = stacked(part[h * z.half : (h + 1) * z.half]).astype(BF16)

            @pl.when(slab // per_half != y_lo)
            def _():
                q = slab % per_half
                send(pbuf.at[slab], prec.at[q], py_s.at[q], py_r.at[q], dp=other).start()

    for q in range(per_half):
        send(pbuf.at[q], prec.at[q], py_s.at[q], py_r.at[q], dp=other).wait_recv()
        for h in range(2):
            both = pbuf[y_lo * per_half + q, h].astype(F32) + prec[q, h].astype(F32)
            to = 2 * q + h
            ssend[to] = both.astype(BF16)

            @pl.when(to != my_z)
            def _():
                k = (to - my_z + z.nz) % z.nz
                send(
                    ssend.at[to], zrec.at[my_z], rz_s.at[k], rz_r.at[k], dp=y_lo * z.nz + to
                ).start()

    for copy in to_other:
        copy.wait_recv()
    for slab in range(z.nx):
        pair = [hbuf[2 * slab + h].astype(F32) for h in range(2)]
        for side in range(2):
            piece = jnp.concatenate([p[side * z.half : (side + 1) * z.half] for p in pair], axis=0)
            hall[slab, :, side * piece.shape[1] : (side + 1) * piece.shape[1]] = piece.astype(BF16)
    rows_all = dbuf[...].reshape(z.nx * z.rows, dbuf.shape[2])
    tile = min(256, gd_ref.shape[1])

    def columns(n, carry):
        at = pl.ds(pl.multiple_of(n * tile, tile), tile)
        kept = hall[:, :, at].reshape(z.nx * z.rows, tile)
        full = lax.dot_general(
            rows_all, kept, (((0,), (0,)), ((), ())), preferred_element_type=F32
        )
        gd_ref[:, at] = full[:width].astype(BF16)
        return carry

    lax.fori_loop(0, gd_ref.shape[1] // tile, columns, 0)

    total = ssend[my_z].astype(F32)
    for k in range(1, z.nz):
        back = z.nz - k
        send(ssend.at[0], zrec.at[0], rz_s.at[k], rz_r.at[k], dp=at_z(k)).wait_recv()
        total = total + zrec[(my_z + back) % z.nz].astype(F32)
    fsend[...] = (total * moved).astype(BF16)
    last = send(fsend, frec, fx_s, fx_r, expert=opposite)
    last.start()
    hg_ref[0] = total * (1.0 - moved)
    last.wait_recv()
    hg_ref[1] = frec[...].astype(F32)

    for copy in to_y + to_core + [to_partner] + to_z + to_other + to_x + [last]:
        copy.wait_send()
    for q in range(per_half):
        send(pbuf.at[q], prec.at[q], py_s.at[q], py_r.at[q], dp=other).wait_send()
    for k in range(1, z.nz):
        send(ssend.at[0], zrec.at[0], rz_s.at[k], rz_r.at[k], dp=at_z(k)).wait_send()


def hidden_of(stored):
    width = stored.shape[-1] // 2
    gate_part = stored[..., :width].astype(F32)
    up_part = stored[..., width:].astype(F32)
    return (gate_part * jax.nn.sigmoid(gate_part) * up_part).astype(BF16)


def swiglu_back(hidden_grad, stored):
    width = stored.shape[-1] // 2
    gate_part = stored[..., :width].astype(F32)
    up_part = stored[..., width:].astype(F32)
    sigmoid_v = jax.nn.sigmoid(gate_part)
    gate_grad = hidden_grad * up_part * sigmoid_v * (1.0 + gate_part * (1.0 - sigmoid_v))
    up_grad = hidden_grad * gate_part * sigmoid_v
    return jnp.concatenate([gate_grad, up_grad], axis=-1).astype(BF16)


def on_device(z, out_grad, gate_weight, expert_ids, replicated, down_weight, pre_act):
    tokens, width = out_grad.shape
    hidden_width = pre_act.shape[3] // 2
    half_lanes = hidden_width // 2
    share, myself = lax.axis_index("dp"), lax.axis_index("expert")

    experts = jnp.arange(z.experts, dtype=jnp.int32)
    named = jnp.any(expert_ids[:, :, None] == experts, axis=1)
    order = jnp.arange(tokens)
    earlier = (order[None, :] < order[:, None]).astype(BF16)
    ranks = 1.0 + jnp.dot(earlier, named.astype(BF16), preferred_element_type=F32)
    ranks = jnp.where(named, ranks, 0.0).astype(BF16)
    high = lax.reduce_precision(gate_weight, 8, 7)
    middle = lax.reduce_precision(gate_weight - high, 8, 7)
    low = gate_weight - high - middle
    table = up_to(width + z.experts, LANES)
    about = jnp.concatenate([expert_ids.astype(F32), high, middle, low], axis=1).astype(BF16)
    fill = jnp.zeros((tokens, table - width - z.experts), BF16)
    message = jnp.concatenate([out_grad, ranks, fill, about], axis=1)
    message = jnp.pad(message, ((0, 0), (0, table + LANES - message.shape[1])))

    hidden = jnp.pad(hidden_of(pre_act[0]), ((0, 0), (0, z.half - z.share_rows), (0, 0)))
    hidden = hidden.reshape(2, z.half, 2, half_lanes).swapaxes(1, 2).reshape(2, z.rows, half_lanes)
    inside = jnp.arange(z.rows) % z.half
    source = share * z.per_share + inside // CAP
    moved = (source % 2 == 1) & (inside < z.share_rows) & (replicated[myself] == 1)
    moved = jnp.broadcast_to(moved.astype(F32)[:, None], (z.rows, LANES))
    weight = jnp.swapaxes(down_weight[0], 0, 1)
    wants = jnp.asarray(row_wants(z, tokens))

    chunk = (z.rows, half_lanes)
    dma = pltpu.SemaphoreType.DMA
    gd, hg = pl.pallas_call(
        functools.partial(kernel, z),
        out_shape=(
            jax.ShapeDtypeStruct((width, hidden_width), BF16),
            jax.ShapeDtypeStruct((2,) + chunk, F32),
        ),
        in_specs=[pl.BlockSpec(memory_space=pltpu.VMEM)] * 5,
        out_specs=(pl.BlockSpec(memory_space=pltpu.VMEM),) * 2,
        scratch_shapes=[
            pltpu.VMEM((z.slab, tokens, table + LANES), BF16),
            pltpu.VMEM(chunk, BF16),
            pltpu.VMEM((z.dp,) + chunk, BF16),
            pltpu.VMEM((z.nx, z.rows, hidden_width), BF16),
            pltpu.VMEM((z.nx, z.rows, table), BF16),
            pltpu.VMEM((z.nx, z.rows, table), BF16),
            pltpu.VMEM((z.nx, 2) + chunk, BF16),
            pltpu.VMEM((z.nx // 2, 2) + chunk, BF16),
            pltpu.VMEM((z.nz,) + chunk, BF16),
            pltpu.VMEM((z.nz,) + chunk, BF16),
            pltpu.VMEM(chunk, BF16),
            pltpu.VMEM(chunk, BF16),
            dma((max(z.ny, 2),)), dma((max(z.ny, 2),)), dma((z.ny,)), dma((z.ny,)), dma, dma,
            dma((z.nz,)), dma((z.nz,)), dma((z.nz,)), dma((z.nz,)),
            dma((z.nx,)), dma((z.nx,)), dma((z.nx // 2,)), dma((z.nx // 2,)),
            dma((z.nz,)), dma((z.nz,)), dma, dma,
        ],
        compiler_params=pltpu.CompilerParams(
            collective_id=0, has_side_effects=True, vmem_limit_bytes=40 << 20
        ),
    )(message, hidden, moved, wants, weight)

    hg = hg.reshape(2, 2, z.half, half_lanes)[:, :, : z.share_rows]
    hg = hg.swapaxes(1, 2).reshape(2, z.share_rows, hidden_width)
    return (jnp.swapaxes(gd, 0, 1)[None], swiglu_back(hg, pre_act[0])[None])


def solution(mesh):
    in_specs = (
        P("expert", "dp"),
        P("expert", None),
        P("expert", None),
        P(),
        P("expert", None, "dp"),
        P("expert", None, "dp", None),
    )
    out_specs = (P("expert", None, "dp"), P("expert", None, "dp", None))
    return jax.shard_map(
        functools.partial(on_device, Sizes(mesh)),
        mesh=mesh, in_specs=in_specs, out_specs=out_specs, check_vma=False,
    )
```

```python
import functools

import jax
import jax.numpy as jnp
import numpy as np
from jax import lax
from jax.experimental import pallas as pl
from jax.experimental.pallas import tpu as pltpu
from jax.sharding import PartitionSpec as P

F32, BF16 = jnp.float32, jnp.bfloat16
CAP = 9
LANES = 128


def up_to(value, step):
    return -(-value // step) * step


class Sizes:
    def __init__(self, mesh):
        self.dp, self.experts = mesh.shape["dp"], mesh.shape["expert"]
        self.nz = self.dp // 2
        self.nx = self.nz
        self.ny = self.experts // (2 * self.nx)
        self.slab = 2 * self.ny
        self.per_share = self.experts // self.dp
        self.share_rows = self.per_share * CAP
        self.half = up_to(self.share_rows, 8)
        self.rows = 2 * self.half


def share_order(z):
    return list(range(1, z.per_share, 2)) + list(range(0, z.per_share, 2))


def packing(width):
    blocks = width // LANES
    return blocks, up_to(blocks * CAP + (CAP + 1) // 2, 16)


def packed_wants(tokens, width):
    blocks, rows = packing(width)
    wants = np.full((rows, up_to((blocks + 2) * tokens, LANES)), -1.0, np.float32)
    for r in range(CAP):
        for b in range(blocks):
            wants[b * CAP + r, b * tokens : (b + 1) * tokens] = r + 1
        side = blocks + r % 2
        wants[blocks * CAP + r // 2, side * tokens : (side + 1) * tokens] = r + 1
    return wants


def unpacking(z, width):
    blocks, rows = packing(width)
    taken = np.zeros((blocks + 2, z.rows, z.slab * rows), np.float32)
    for h in range(2):
        for n, source in enumerate(share_order(z)):
            for r in range(CAP):
                at, start = h * z.half + n * CAP + r, (h * z.per_share + source) * rows
                for b in range(blocks):
                    taken[b, at, start + b * CAP + r] = 1
                taken[blocks + r % 2, at, start + blocks * CAP + r // 2] = 1
    return taken.reshape(-1, z.slab * rows)


def stacked(value):
    width = value.shape[1] // 2
    return jnp.concatenate([value[:, :width], value[:, width:]], axis=0)


def kernel(
    z,
    tok_ref, tab_ref, hid_ref, moved_ref, wants_ref, take_ref, wt_ref,
    gd_ref, hg_ref,
    sbuf, abuf, theirs, hbuf, hall, dbuf, pbuf, prec, ssend, zrec, fsend, frec,
    th_s, th_r, hz_s, hz_r, hy_s, hy_r,
    dx_s, dx_r, py_s, py_r, rz_s, rz_r, fx_s, fx_r,
):
    dp, ex = lax.axis_index("dp"), lax.axis_index("expert")
    y_lo, my_z = dp // z.nz, dp % z.nz
    my_x, yc = ex // z.slab, ex % z.slab

    def at_z(k):
        return y_lo * z.nz + (my_z + k) % z.nz

    def at_x(k):
        return ((my_x + k) % z.nx) * z.slab + yc

    other = (1 - y_lo) * z.nz + my_z
    opposite = at_x(z.nx // 2)

    def send(src, dst, s, r, **where):
        copy = pltpu.make_async_remote_copy(
            src_ref=src, dst_ref=dst, send_sem=s, recv_sem=r,
            device_id=where, device_id_type=pl.DeviceIdType.MESH,
        )
        return copy

    barrier = pltpu.get_barrier_semaphore()
    def greet(**where):
        pl.semaphore_signal(barrier, inc=1, device_id=where, device_id_type=pl.DeviceIdType.MESH)

    def greet_expert(k, carry):
        greet(expert=(ex + k) % z.experts)
        return carry

    lax.fori_loop(1, z.experts, greet_expert, 0)
    for k in range(1, z.nz):
        greet(dp=at_z(k))
    greet(dp=other)
    pl.semaphore_wait(barrier, z.experts + z.nz - 1)

    to_partner = send(hid_ref.at[1], theirs, th_s, th_r, expert=opposite)
    to_partner.start()

    message = sbuf.shape[2:]
    width = wt_ref.shape[0]
    tokens, wants = tok_ref[...], wants_ref[...]

    def prepare(step):
        x = (my_x + step) % z.nx
        shape = (z.slab,) + wants.shape
        hit = jnp.broadcast_to(tab_ref[0, x][:, None], shape) == wants[None]
        picked = 0.0
        for n in range(1, 4):
            part = jnp.where(hit, jnp.broadcast_to(tab_ref[n, x][:, None], shape), 0.0)
            part = part.reshape(-1, shape[2]).astype(BF16)
            picked = picked + jnp.dot(part, tokens, preferred_element_type=F32)
        sbuf[step] = picked.astype(BF16).reshape(sbuf.shape[1:])
        return x

    def to_slab(n, carry):
        step = 1 + (n + z.nx // 2 - 1) % (z.nx - 1)
        x = prepare(step)

        def one(j, inner):
            send(
                sbuf.at[step, j], abuf.at[my_x, yc], dx_s.at[step], dx_r.at[step],
                expert=x * z.slab + j,
            ).start()
            return inner

        return lax.fori_loop(0, z.slab, one, carry)

    def to_own_slab(m, carry):
        j = (yc + m) % z.slab
        send(
            sbuf.at[0, j], abuf.at[my_x, yc], dx_s.at[0], dx_r.at[0], expert=my_x * z.slab + j
        ).start()
        return carry

    lax.fori_loop(0, z.nx - 1, to_slab, 0)
    prepare(0)
    lax.fori_loop(1, z.slab, to_own_slab, 0)
    abuf[my_x, yc] = sbuf[0, yc]

    moved = jnp.concatenate([moved_ref[...]] * (hbuf.shape[2] // LANES), axis=1)
    to_partner.wait_recv()
    hbuf[dp] = (
        hid_ref[0].astype(F32) * (1.0 - moved) + theirs[...].astype(F32) * moved
    ).astype(BF16)
    to_z = [
        send(hbuf.at[dp], hbuf.at[dp], hz_s.at[k], hz_r.at[k], dp=at_z(k)) for k in range(1, z.nz)
    ]
    for copy in to_z:
        copy.start()
    to_other = [send(hbuf.at[dp], hbuf.at[dp], hy_s.at[0], hy_r.at[0], dp=other)]
    to_other[0].start()

    per_half = z.nx // 2
    for k in range(0, z.nx // 2 + 1):
        for step in (k,) if k in (0, z.nx // 2) else (z.nx - k, k):
            slab = (my_x + step) % z.nx
            back = (z.nx - step) % z.nx
            came = abuf.at[slab] if step else abuf.at[slab, pl.ds(0, z.slab - 1)]
            send(came, came, dx_s.at[back], dx_r.at[back], dp=other).wait_recv()
            arrived = abuf[slab].reshape(z.slab * message[0], message[1])
            taken = jnp.dot(take_ref[...], arrived, preferred_element_type=F32)
            taken = [taken[n * z.rows : (n + 1) * z.rows] for n in range(taken.shape[0] // z.rows)]
            ends = taken[-2] + pltpu.roll(taken[-1], LANES // 2, 1)
            dbuf[slab] = jnp.concatenate(taken[:-2] + [ends], axis=1).astype(BF16)
            part = jnp.dot(dbuf[slab][:, :width], wt_ref[...], preferred_element_type=F32)
            for h in range(2):
                pbuf[slab, h] = stacked(part[h * z.half : (h + 1) * z.half]).astype(BF16)

            @pl.when(slab // per_half != y_lo)
            def _():
                q = slab % per_half
                send(pbuf.at[slab], prec.at[q], py_s.at[q], py_r.at[q], dp=other).start()

    for q in range(per_half):
        send(pbuf.at[q], prec.at[q], py_s.at[q], py_r.at[q], dp=other).wait_recv()
        for h in range(2):
            both = pbuf[y_lo * per_half + q, h].astype(F32) + prec[q, h].astype(F32)
            to = 2 * q + h
            ssend[to] = both.astype(BF16)

            @pl.when(to != my_z)
            def _():
                k = (to - my_z + z.nz) % z.nz
                send(
                    ssend.at[to], zrec.at[my_z], rz_s.at[k], rz_r.at[k], dp=y_lo * z.nz + to
                ).start()

    for k in range(1, z.nz):
        to_z[k - 1].wait_recv()
        slot = at_z(z.nz - k)
        copy = send(hbuf.at[slot], hbuf.at[slot], hy_s.at[k], hy_r.at[k], dp=other)
        copy.start()
        to_other.append(copy)

    total = ssend[my_z].astype(F32)
    for k in range(1, z.nz):
        back = z.nz - k
        send(ssend.at[0], zrec.at[0], rz_s.at[k], rz_r.at[k], dp=at_z(k)).wait_recv()
        total = total + zrec[(my_z + back) % z.nz].astype(F32)
    few = fsend.shape[0] // 2
    going = total * moved
    fsend[...] = jnp.concatenate([going[:few], going[z.half : z.half + few]], axis=0).astype(BF16)
    last = send(fsend, frec, fx_s, fx_r, expert=opposite)
    last.start()
    hg_ref[0] = total - going

    for copy in to_other:
        copy.wait_recv()
    for slab in range(z.nx):
        pair = [hbuf[2 * slab + h].astype(F32) for h in range(2)]
        for side in range(2):
            piece = jnp.concatenate([p[side * z.half : (side + 1) * z.half] for p in pair], axis=0)
            hall[slab, :, side * piece.shape[1] : (side + 1) * piece.shape[1]] = piece.astype(BF16)
    rows_all = dbuf[...].reshape(z.nx * z.rows, dbuf.shape[2])
    tile = min(256, gd_ref.shape[1])

    def columns(n, carry):
        at = pl.ds(pl.multiple_of(n * tile, tile), tile)
        kept = hall[:, :, at].reshape(z.nx * z.rows, tile)
        full = lax.dot_general(
            rows_all, kept, (((0,), (0,)), ((), ())), preferred_element_type=F32
        )
        gd_ref[:, at] = full[:width].astype(BF16)
        return carry

    lax.fori_loop(0, gd_ref.shape[1] // tile, columns, 0)

    last.wait_recv()
    came = frec[...].astype(F32)
    empty = jnp.zeros((z.half - few, came.shape[1]), F32)
    hg_ref[1] = jnp.concatenate([came[:few], empty, came[few:], empty], axis=0)

    for copy in [to_partner] + to_z + to_other + [last]:
        copy.wait_send()
    for step in range(z.nx):
        sent = sbuf.at[step] if step else sbuf.at[0, pl.ds(0, z.slab - 1)]
        send(sent, sent, dx_s.at[step], dx_r.at[step], dp=other).wait_send()
    for q in range(per_half):
        send(pbuf.at[q], prec.at[q], py_s.at[q], py_r.at[q], dp=other).wait_send()
    for k in range(1, z.nz):
        send(ssend.at[0], zrec.at[0], rz_s.at[k], rz_r.at[k], dp=at_z(k)).wait_send()


def hidden_of(stored):
    width = stored.shape[-1] // 2
    gate_part = stored[..., :width].astype(F32)
    up_part = stored[..., width:].astype(F32)
    return (gate_part * jax.nn.sigmoid(gate_part) * up_part).astype(BF16)


def swiglu_back(hidden_grad, stored):
    width = stored.shape[-1] // 2
    gate_part = stored[..., :width].astype(F32)
    up_part = stored[..., width:].astype(F32)
    sigmoid_v = jax.nn.sigmoid(gate_part)
    gate_grad = hidden_grad * up_part * sigmoid_v * (1.0 + gate_part * (1.0 - sigmoid_v))
    up_grad = hidden_grad * gate_part * sigmoid_v
    return jnp.concatenate([gate_grad, up_grad], axis=-1).astype(BF16)


def on_device(z, out_grad, gate_weight, expert_ids, replicated, down_weight, pre_act):
    tokens, width = out_grad.shape
    hidden_width = pre_act.shape[3] // 2
    half_lanes = hidden_width // 2
    myself = lax.axis_index("expert")

    experts = jnp.arange(z.experts, dtype=jnp.int32)
    names = jnp.swapaxes(expert_ids, 0, 1)[None] == experts[:, None, None]
    named = jnp.any(names, axis=1)
    gates = jnp.sum(jnp.where(names, jnp.swapaxes(gate_weight, 0, 1)[None], 0.0), axis=1)
    order = jnp.arange(tokens)
    earlier = (order[:, None] < order[None, :]).astype(BF16)
    ranks = 1.0 + jnp.dot(named.astype(BF16), earlier, preferred_element_type=F32)
    ranks = jnp.where(named, ranks, 0.0)
    high = lax.reduce_precision(gates, 8, 7)
    middle = lax.reduce_precision(gates - high, 8, 7)
    wants = packed_wants(tokens, width)
    blocks, message_rows = packing(width)
    table = jnp.tile(jnp.stack([ranks, high, middle, gates - high - middle]), (1, 1, blocks + 2))
    table = jnp.pad(table, ((0, 0), (0, 0), (0, wants.shape[1] - table.shape[2])))
    table = table.reshape(4, z.nx, z.slab, wants.shape[1])
    ends = out_grad[:, blocks * LANES :]
    beside = LANES - ends.shape[1]
    picks = [out_grad[:, b * LANES : (b + 1) * LANES] for b in range(blocks)]
    picks += [jnp.pad(ends, ((0, 0), (0, beside))), jnp.pad(ends, ((0, 0), (beside, 0)))]
    picks = jnp.concatenate(picks)
    picks = jnp.pad(picks, ((0, wants.shape[1] - picks.shape[0]), (0, 0)))

    hidden = hidden_of(pre_act[0]).reshape(2, z.per_share, CAP, hidden_width)
    hidden = jnp.concatenate([hidden[:, n] for n in share_order(z)], axis=1)
    hidden = jnp.pad(hidden, ((0, 0), (0, z.half - z.share_rows), (0, 0)))
    hidden = hidden.reshape(2, z.half, 2, half_lanes).swapaxes(1, 2).reshape(2, z.rows, half_lanes)
    odd_rows = z.per_share // 2 * CAP
    inside = jnp.arange(z.rows) % z.half
    moved = (inside < odd_rows) & (replicated[myself] == 1)
    moved = jnp.broadcast_to(moved.astype(F32)[:, None], (z.rows, LANES))
    weight = jnp.swapaxes(down_weight[0], 0, 1)
    take = jnp.asarray(unpacking(z, width), BF16)
    few = (2 * up_to(odd_rows, 8), half_lanes)

    chunk = (z.rows, half_lanes)
    dma = pltpu.SemaphoreType.DMA
    gd, hg = pl.pallas_call(
        functools.partial(kernel, z),
        out_shape=(
            jax.ShapeDtypeStruct((width, hidden_width), BF16),
            jax.ShapeDtypeStruct((2,) + chunk, F32),
        ),
        in_specs=[pl.BlockSpec(memory_space=pltpu.VMEM)] * 7,
        out_specs=(pl.BlockSpec(memory_space=pltpu.VMEM),) * 2,
        scratch_shapes=[
            pltpu.VMEM((z.nx, z.slab, message_rows, LANES), BF16),
            pltpu.VMEM((z.nx, z.slab, message_rows, LANES), BF16),
            pltpu.VMEM(chunk, BF16),
            pltpu.VMEM((z.dp,) + chunk, BF16),
            pltpu.VMEM((z.nx, z.rows, hidden_width), BF16),
            pltpu.VMEM((z.nx, z.rows, up_to(width, LANES)), BF16),
            pltpu.VMEM((z.nx, 2) + chunk, BF16),
            pltpu.VMEM((z.nx // 2, 2) + chunk, BF16),
            pltpu.VMEM((z.nz,) + chunk, BF16),
            pltpu.VMEM((z.nz,) + chunk, BF16),
            pltpu.VMEM(few, BF16),
            pltpu.VMEM(few, BF16),
            dma, dma,
            dma((z.nz,)), dma((z.nz,)), dma((z.nz,)), dma((z.nz,)),
            dma((z.nx,)), dma((z.nx,)), dma((z.nx // 2,)), dma((z.nx // 2,)),
            dma((z.nz,)), dma((z.nz,)), dma, dma,
        ],
        compiler_params=pltpu.CompilerParams(
            collective_id=0, has_side_effects=True, vmem_limit_bytes=40 << 20
        ),
    )(picks, table, hidden, moved, jnp.asarray(wants), take, weight)

    hg = hg.reshape(2, 2, z.half, half_lanes)[:, :, : z.share_rows]
    hg = hg.reshape(2, 2, z.per_share, CAP, half_lanes)
    placed = share_order(z)
    hg = jnp.concatenate([hg[:, :, placed.index(n)] for n in range(z.per_share)], axis=2)
    hg = hg.swapaxes(1, 2).reshape(2, z.share_rows, hidden_width)
    return (jnp.swapaxes(gd, 0, 1)[None], swiglu_back(hg, pre_act[0])[None])


def solution(mesh):
    in_specs = (
        P("expert", "dp"),
        P("expert", None),
        P("expert", None),
        P(),
        P("expert", None, "dp"),
        P("expert", None, "dp", None),
    )
    out_specs = (P("expert", None, "dp"), P("expert", None, "dp", None))
    return jax.shard_map(
        functools.partial(on_device, Sizes(mesh)),
        mesh=mesh, in_specs=in_specs, out_specs=out_specs, check_vma=False,
    )
```

```python
import functools

import jax
import jax.numpy as jnp
import numpy as np
from jax import lax
from jax.experimental import pallas as pl
from jax.experimental.pallas import tpu as pltpu
from jax.sharding import PartitionSpec as P

F32, BF16 = jnp.float32, jnp.bfloat16
CAP = 9
LANES = 128


def up_to(value, step):
    return -(-value // step) * step


class Sizes:
    def __init__(self, mesh):
        self.dp, self.experts = mesh.shape["dp"], mesh.shape["expert"]
        self.nz = self.dp // 2
        self.nx = self.nz
        self.ny = self.experts // (2 * self.nx)
        self.slab = 2 * self.ny
        self.per_share = self.experts // self.dp
        self.share_rows = self.per_share * CAP
        self.half = up_to(self.share_rows, 8)
        self.rows = 2 * self.half


def share_order(z):
    return list(range(1, z.per_share, 2)) + list(range(0, z.per_share, 2))


def packing(width):
    blocks = width // LANES
    return blocks, up_to(blocks * CAP + (CAP + 1) // 2, 16)


def packed_wants(tokens, width):
    blocks, rows = packing(width)
    wants = np.full((rows, up_to((blocks + 2) * tokens, LANES)), -1.0, np.float32)
    for r in range(CAP):
        for b in range(blocks):
            wants[b * CAP + r, b * tokens : (b + 1) * tokens] = r + 1
        side = blocks + r % 2
        wants[blocks * CAP + r // 2, side * tokens : (side + 1) * tokens] = r + 1
    return wants


def unpacking(z, width):
    blocks, rows = packing(width)
    taken = np.zeros((blocks + 2, z.rows, z.slab * rows), np.float32)
    for h in range(2):
        for n, source in enumerate(share_order(z)):
            for r in range(CAP):
                at, start = h * z.half + n * CAP + r, (h * z.per_share + source) * rows
                for b in range(blocks):
                    taken[b, at, start + b * CAP + r] = 1
                taken[blocks + r % 2, at, start + blocks * CAP + r // 2] = 1
    return taken.reshape(-1, z.slab * rows)


def stacked(value):
    width = value.shape[1] // 2
    return jnp.concatenate([value[:, :width], value[:, width:]], axis=0)


def kernel(
    z,
    og_ref, id_ref, gate_ref, rep_ref, hid_ref, wants_ref, spread_ref, take_ref, wt_ref,
    gd_ref, hg_ref,
    tok_ref, end_ref, tab_ref, sbuf, abuf, theirs, hbuf, hall, dbuf, pbuf, prec, ssend, zrec, fsend, frec,
    th_s, th_r, hz_s, hz_r, hy_s, hy_r,
    dx_s, dx_r, py_s, py_r, rz_s, rz_r, fx_s, fx_r,
):
    dp, ex = lax.axis_index("dp"), lax.axis_index("expert")
    y_lo, my_z = dp // z.nz, dp % z.nz
    my_x, yc = ex // z.slab, ex % z.slab

    def at_z(k):
        return y_lo * z.nz + (my_z + k) % z.nz

    def at_x(k):
        return ((my_x + k) % z.nx) * z.slab + yc

    other = (1 - y_lo) * z.nz + my_z
    opposite = at_x(z.nx // 2)

    def send(src, dst, s, r, **where):
        copy = pltpu.make_async_remote_copy(
            src_ref=src, dst_ref=dst, send_sem=s, recv_sem=r,
            device_id=where, device_id_type=pl.DeviceIdType.MESH,
        )
        return copy

    barrier = pltpu.get_barrier_semaphore()

    def greet(**where):
        pl.semaphore_signal(barrier, inc=1, device_id=where, device_id_type=pl.DeviceIdType.MESH)

    def greet_expert(k, carry):
        greet(expert=(ex + k) % z.experts)
        return carry

    lax.fori_loop(1, z.experts, greet_expert, 0)
    for k in range(1, z.nz):
        greet(dp=at_z(k))
    greet(dp=other)
    count = og_ref.shape[0]
    table = (z.experts, count)
    expert = lax.broadcasted_iota(jnp.int32, table, 0)
    named, gates = jnp.zeros(table, F32), jnp.zeros(table, F32)
    for k in range(id_ref.shape[0]):
        here = jnp.broadcast_to(id_ref[k : k + 1, :], table) == expert
        named = jnp.where(here, 1.0, named)
        gates = jnp.where(here, jnp.broadcast_to(gate_ref[k : k + 1, :], table), gates)
    order = [lax.broadcasted_iota(jnp.int32, (count, count), n) for n in range(2)]
    earlier = jnp.where(order[0] < order[1], 1.0, 0.0).astype(BF16)
    ranks = named * (1.0 + jnp.dot(named.astype(BF16), earlier, preferred_element_type=F32))
    high = gates.astype(BF16)
    middle = (gates - high.astype(F32)).astype(BF16)
    low = (gates - high.astype(F32) - middle.astype(F32)).astype(BF16)
    for n, part in enumerate((ranks.astype(BF16), high, middle, low)):
        wide = jnp.dot(part, spread_ref[...], preferred_element_type=F32)
        tab_ref[n] = wide.reshape(tab_ref.shape[1:])

    blocks = og_ref.shape[1] // LANES
    tok_ref[...] = jnp.zeros_like(tok_ref)
    end_ref[...] = jnp.zeros_like(end_ref)
    for b in range(blocks):
        tok_ref[b * count : (b + 1) * count] = og_ref[:, b * LANES : (b + 1) * LANES]
    ends = og_ref[:, blocks * LANES :].astype(F32)
    end_ref[:, : ends.shape[1]] = ends
    ends = end_ref[...]
    tok_ref[blocks * count : (blocks + 1) * count] = ends.astype(BF16)
    ends = pltpu.roll(ends, LANES // 2, 1)
    tok_ref[(blocks + 1) * count : (blocks + 2) * count] = ends.astype(BF16)

    message = sbuf.shape[2:]
    width = wt_ref.shape[0]
    tokens, wants = tok_ref[...], wants_ref[...]

    def prepare(step, carry):
        x = (my_x + step) % z.nx
        shape = (z.slab,) + wants.shape
        hit = jnp.broadcast_to(tab_ref[0, x][:, None], shape) == wants[None]
        picked = 0.0
        for n in range(1, 4):
            part = jnp.where(hit, jnp.broadcast_to(tab_ref[n, x][:, None], shape), 0.0)
            part = part.reshape(-1, shape[2]).astype(BF16)
            picked = picked + jnp.dot(part, tokens, preferred_element_type=F32)
        sbuf[step] = picked.astype(BF16).reshape(sbuf.shape[1:])
        return carry

    lax.fori_loop(0, z.nx, prepare, 0)
    pl.semaphore_wait(barrier, z.experts + z.nz - 1)

    to_partner = send(hid_ref.at[1], theirs, th_s, th_r, expert=opposite)
    to_partner.start()

    def to_slab(n, carry):
        step = 1 + (n + z.nx // 2 - 1) % (z.nx - 1)
        x = (my_x + step) % z.nx

        def one(j, inner):
            send(
                sbuf.at[step, j], abuf.at[my_x, yc], dx_s.at[step], dx_r.at[step],
                expert=x * z.slab + j,
            ).start()
            return inner

        return lax.fori_loop(0, z.slab, one, carry)

    def to_own_slab(m, carry):
        j = (yc + m) % z.slab
        send(
            sbuf.at[0, j], abuf.at[my_x, yc], dx_s.at[0], dx_r.at[0], expert=my_x * z.slab + j
        ).start()
        return carry

    lax.fori_loop(0, z.nx - 1, to_slab, 0)
    lax.fori_loop(1, z.slab, to_own_slab, 0)
    abuf[my_x, yc] = sbuf[0, yc]

    lane = lax.broadcasted_iota(jnp.int32, rep_ref.shape, 1)
    has_second = jnp.sum(jnp.where(lane == ex, rep_ref[...], 0), axis=1, keepdims=True)
    row = lax.broadcasted_iota(jnp.int32, theirs.shape, 0)
    inside = jnp.where(row < z.half, row, row - z.half)
    second = jnp.broadcast_to(has_second, theirs.shape) == 1
    moved = jnp.where((inside < z.per_share // 2 * CAP) & second, 1.0, 0.0)
    to_partner.wait_recv()
    hbuf[dp] = (
        hid_ref[0].astype(F32) * (1.0 - moved) + theirs[...].astype(F32) * moved
    ).astype(BF16)
    to_z = [
        send(hbuf.at[dp], hbuf.at[dp], hz_s.at[k], hz_r.at[k], dp=at_z(k)) for k in range(1, z.nz)
    ]
    for copy in to_z:
        copy.start()
    to_other = [send(hbuf.at[dp], hbuf.at[dp], hy_s.at[0], hy_r.at[0], dp=other)]
    to_other[0].start()

    per_half = z.nx // 2
    for k in range(0, z.nx // 2 + 1):
        for step in (k,) if k in (0, z.nx // 2) else (z.nx - k, k):
            slab = (my_x + step) % z.nx
            back = (z.nx - step) % z.nx
            came = abuf.at[slab] if step else abuf.at[slab, pl.ds(0, z.slab - 1)]
            send(came, came, dx_s.at[back], dx_r.at[back], dp=other).wait_recv()
            arrived = abuf[slab].reshape(z.slab * message[0], message[1])
            taken = jnp.dot(take_ref[...], arrived, preferred_element_type=F32)
            taken = [taken[n * z.rows : (n + 1) * z.rows] for n in range(taken.shape[0] // z.rows)]
            ends = taken[-2] + pltpu.roll(taken[-1], LANES // 2, 1)
            dbuf[slab] = jnp.concatenate(taken[:-2] + [ends], axis=1).astype(BF16)
            part = jnp.dot(dbuf[slab][:, :width], wt_ref[...], preferred_element_type=F32)
            for h in range(2):
                pbuf[slab, h] = stacked(part[h * z.half : (h + 1) * z.half]).astype(BF16)

            @pl.when(slab // per_half != y_lo)
            def _():
                q = slab % per_half
                send(pbuf.at[slab], prec.at[q], py_s.at[q], py_r.at[q], dp=other).start()

    for q in range(per_half):
        send(pbuf.at[q], prec.at[q], py_s.at[q], py_r.at[q], dp=other).wait_recv()
        for h in range(2):
            both = pbuf[y_lo * per_half + q, h].astype(F32) + prec[q, h].astype(F32)
            to = 2 * q + h
            ssend[to] = both.astype(BF16)

            @pl.when(to != my_z)
            def _():
                k = (to - my_z + z.nz) % z.nz
                send(
                    ssend.at[to], zrec.at[my_z], rz_s.at[k], rz_r.at[k], dp=y_lo * z.nz + to
                ).start()

    for k in range(1, z.nz):
        to_z[k - 1].wait_recv()
        slot = at_z(z.nz - k)
        copy = send(hbuf.at[slot], hbuf.at[slot], hy_s.at[k], hy_r.at[k], dp=other)
        copy.start()
        to_other.append(copy)

    total = ssend[my_z].astype(F32)
    for k in range(1, z.nz):
        back = z.nz - k
        send(ssend.at[0], zrec.at[0], rz_s.at[k], rz_r.at[k], dp=at_z(k)).wait_recv()
        total = total + zrec[(my_z + back) % z.nz].astype(F32)
    few = fsend.shape[0] // 2
    going = total * moved
    fsend[...] = jnp.concatenate([going[:few], going[z.half : z.half + few]], axis=0).astype(BF16)
    last = send(fsend, frec, fx_s, fx_r, expert=opposite)
    last.start()
    hg_ref[0] = total - going

    for copy in to_other:
        copy.wait_recv()
    for slab in range(z.nx):
        pair = [hbuf[2 * slab + h].astype(F32) for h in range(2)]
        for side in range(2):
            piece = jnp.concatenate([p[side * z.half : (side + 1) * z.half] for p in pair], axis=0)
            hall[slab, :, side * piece.shape[1] : (side + 1) * piece.shape[1]] = piece.astype(BF16)
    rows_all = dbuf[...].reshape(z.nx * z.rows, dbuf.shape[2])
    tile = min(256, gd_ref.shape[1])

    def columns(n, carry):
        at = pl.ds(pl.multiple_of(n * tile, tile), tile)
        kept = hall[:, :, at].reshape(z.nx * z.rows, tile)
        full = lax.dot_general(
            rows_all, kept, (((0,), (0,)), ((), ())), preferred_element_type=F32
        )
        gd_ref[:, at] = full[:width].astype(BF16)
        return carry

    lax.fori_loop(0, gd_ref.shape[1] // tile, columns, 0)

    last.wait_recv()
    came = frec[...].astype(F32)
    empty = jnp.zeros((z.half - few, came.shape[1]), F32)
    hg_ref[1] = jnp.concatenate([came[:few], empty, came[few:], empty], axis=0)

    for copy in [to_partner] + to_z + to_other + [last]:
        copy.wait_send()
    for step in range(z.nx):
        sent = sbuf.at[step] if step else sbuf.at[0, pl.ds(0, z.slab - 1)]
        send(sent, sent, dx_s.at[step], dx_r.at[step], dp=other).wait_send()
    for q in range(per_half):
        send(pbuf.at[q], prec.at[q], py_s.at[q], py_r.at[q], dp=other).wait_send()
    for k in range(1, z.nz):
        send(ssend.at[0], zrec.at[0], rz_s.at[k], rz_r.at[k], dp=at_z(k)).wait_send()


def hidden_of(stored):
    width = stored.shape[-1] // 2
    gate_part = stored[..., :width].astype(F32)
    up_part = stored[..., width:].astype(F32)
    return (gate_part * jax.nn.sigmoid(gate_part) * up_part).astype(BF16)


def swiglu_back(hidden_grad, stored):
    width = stored.shape[-1] // 2
    gate_part = stored[..., :width].astype(F32)
    up_part = stored[..., width:].astype(F32)
    sigmoid_v = jax.nn.sigmoid(gate_part)
    gate_grad = hidden_grad * up_part * sigmoid_v * (1.0 + gate_part * (1.0 - sigmoid_v))
    up_grad = hidden_grad * gate_part * sigmoid_v
    return jnp.concatenate([gate_grad, up_grad], axis=-1).astype(BF16)


def on_device(z, out_grad, gate_weight, expert_ids, replicated, down_weight, pre_act):
    tokens, width = out_grad.shape
    hidden_width = pre_act.shape[3] // 2
    half_lanes = hidden_width // 2

    wants = packed_wants(tokens, width)
    blocks, message_rows = packing(width)
    spread = np.zeros((tokens, wants.shape[1]), np.float32)
    for b in range(blocks + 2):
        spread[:, b * tokens : (b + 1) * tokens] = np.eye(tokens)

    hidden = hidden_of(pre_act[0]).reshape(2, z.per_share, CAP, hidden_width)
    hidden = jnp.concatenate([hidden[:, n] for n in share_order(z)], axis=1)
    hidden = jnp.pad(hidden, ((0, 0), (0, z.half - z.share_rows), (0, 0)))
    hidden = hidden.reshape(2, z.half, 2, half_lanes).swapaxes(1, 2).reshape(2, z.rows, half_lanes)
    odd_rows = z.per_share // 2 * CAP
    weight = jnp.swapaxes(down_weight[0], 0, 1)
    take = jnp.asarray(unpacking(z, width), BF16)
    few = (2 * up_to(odd_rows, 8), half_lanes)

    chunk = (z.rows, half_lanes)
    dma = pltpu.SemaphoreType.DMA
    gd, hg = pl.pallas_call(
        functools.partial(kernel, z),
        out_shape=(
            jax.ShapeDtypeStruct((width, hidden_width), BF16),
            jax.ShapeDtypeStruct((2,) + chunk, F32),
        ),
        in_specs=[pl.BlockSpec(memory_space=pltpu.VMEM)] * 9,
        out_specs=(pl.BlockSpec(memory_space=pltpu.VMEM),) * 2,
        scratch_shapes=[
            pltpu.VMEM((wants.shape[1], LANES), BF16),
            pltpu.VMEM((tokens, LANES), F32),
            pltpu.VMEM((4, z.nx, z.slab, wants.shape[1]), F32),
            pltpu.VMEM((z.nx, z.slab, message_rows, LANES), BF16),
            pltpu.VMEM((z.nx, z.slab, message_rows, LANES), BF16),
            pltpu.VMEM(chunk, BF16),
            pltpu.VMEM((z.dp,) + chunk, BF16),
            pltpu.VMEM((z.nx, z.rows, hidden_width), BF16),
            pltpu.VMEM((z.nx, z.rows, up_to(width, LANES)), BF16),
            pltpu.VMEM((z.nx, 2) + chunk, BF16),
            pltpu.VMEM((z.nx // 2, 2) + chunk, BF16),
            pltpu.VMEM((z.nz,) + chunk, BF16),
            pltpu.VMEM((z.nz,) + chunk, BF16),
            pltpu.VMEM(few, BF16),
            pltpu.VMEM(few, BF16),
            dma, dma,
            dma((z.nz,)), dma((z.nz,)), dma((z.nz,)), dma((z.nz,)),
            dma((z.nx,)), dma((z.nx,)), dma((z.nx // 2,)), dma((z.nx // 2,)),
            dma((z.nz,)), dma((z.nz,)), dma, dma,
        ],
        compiler_params=pltpu.CompilerParams(
            collective_id=0, has_side_effects=True, vmem_limit_bytes=40 << 20
        ),
    )(
        out_grad, jnp.swapaxes(expert_ids, 0, 1), jnp.swapaxes(gate_weight, 0, 1), replicated[None],
        hidden, jnp.asarray(wants), jnp.asarray(spread, BF16), take, weight,
    )

    hg = hg.reshape(2, 2, z.half, half_lanes)[:, :, : z.share_rows]
    hg = hg.reshape(2, 2, z.per_share, CAP, half_lanes)
    placed = share_order(z)
    hg = jnp.concatenate([hg[:, :, placed.index(n)] for n in range(z.per_share)], axis=2)
    hg = hg.swapaxes(1, 2).reshape(2, z.share_rows, hidden_width)
    return (jnp.swapaxes(gd, 0, 1)[None], swiglu_back(hg, pre_act[0])[None])


def solution(mesh):
    in_specs = (
        P("expert", "dp"),
        P("expert", None),
        P("expert", None),
        P(),
        P("expert", None, "dp"),
        P("expert", None, "dp", None),
    )
    out_specs = (P("expert", None, "dp"), P("expert", None, "dp", None))
    return jax.shard_map(
        functools.partial(on_device, Sizes(mesh)),
        mesh=mesh, in_specs=in_specs, out_specs=out_specs, check_vma=False,
    )
```

```python
import functools

import jax
import jax.numpy as jnp
import numpy as np
from jax import lax
from jax.experimental import pallas as pl
from jax.experimental.pallas import tpu as pltpu
from jax.sharding import PartitionSpec as P

F32, BF16 = jnp.float32, jnp.bfloat16
CAP = 9
LANES = 128


def up_to(value, step):
    return -(-value // step) * step


class Sizes:
    def __init__(self, mesh):
        self.dp, self.experts = mesh.shape["dp"], mesh.shape["expert"]
        self.nz = self.dp // 2
        self.nx = self.nz
        self.ny = self.experts // (2 * self.nx)
        self.slab = 2 * self.ny
        self.per_share = self.experts // self.dp
        self.share_rows = self.per_share * CAP
        self.half = up_to(self.share_rows, 8)
        self.rows = 2 * self.half


def share_order(z):
    return list(range(1, z.per_share, 2)) + list(range(0, z.per_share, 2))


def packing(width):
    blocks = width // LANES
    return blocks, up_to(blocks * CAP + (CAP + 1) // 2, 16)


def packed_wants(tokens, width):
    blocks, rows = packing(width)
    wants = np.full((rows, up_to((blocks + 2) * tokens, LANES)), -1.0, np.float32)
    for r in range(CAP):
        for b in range(blocks):
            wants[b * CAP + r, b * tokens : (b + 1) * tokens] = r + 1
        side = blocks + r % 2
        wants[blocks * CAP + r // 2, side * tokens : (side + 1) * tokens] = r + 1
    return wants


def unpacking(z, width):
    blocks, rows = packing(width)
    taken = np.zeros((blocks + 2, z.rows, z.slab * rows), np.float32)
    for h in range(2):
        for n, source in enumerate(share_order(z)):
            for r in range(CAP):
                at, start = h * z.half + n * CAP + r, (h * z.per_share + source) * rows
                for b in range(blocks):
                    taken[b, at, start + b * CAP + r] = 1
                taken[blocks + r % 2, at, start + blocks * CAP + r // 2] = 1
    return taken.reshape(-1, z.slab * rows)


def stacked(value):
    width = value.shape[1] // 2
    return jnp.concatenate([value[:, :width], value[:, width:]], axis=0)


def kernel(
    z,
    og_ref, id_ref, gate_ref, rep_ref, hid_ref, wants_ref, spread_ref, take_ref, wt_ref,
    gd_ref, hg_ref,
    tok_ref, end_ref, tab_ref, sbuf, abuf, theirs, hbuf, hall, dbuf, pbuf, prec, ssend, zrec, fsend, frec,
    th_s, th_r, hz_s, hz_r, hy_s, hy_r,
    dx_s, dx_r, py_s, py_r, rz_s, rz_r, fx_s, fx_r,
):
    dp, ex = lax.axis_index("dp"), lax.axis_index("expert")
    y_lo, my_z = dp // z.nz, dp % z.nz
    my_x, yc = ex // z.slab, ex % z.slab

    def at_z(k):
        return y_lo * z.nz + (my_z + k) % z.nz

    def at_x(k):
        return ((my_x + k) % z.nx) * z.slab + yc

    other = (1 - y_lo) * z.nz + my_z
    opposite = at_x(z.nx // 2)

    def send(src, dst, s, r, **where):
        copy = pltpu.make_async_remote_copy(
            src_ref=src, dst_ref=dst, send_sem=s, recv_sem=r,
            device_id=where, device_id_type=pl.DeviceIdType.MESH,
        )
        return copy

    barrier = pltpu.get_barrier_semaphore()

    def greet(**where):
        pl.semaphore_signal(barrier, inc=1, device_id=where, device_id_type=pl.DeviceIdType.MESH)

    def greet_expert(k, carry):
        greet(expert=(ex + k) % z.experts)
        return carry

    lax.fori_loop(1, z.experts, greet_expert, 0)
    for k in range(1, z.nz):
        greet(dp=at_z(k))
    greet(dp=other)
    count = og_ref.shape[0]
    table = (z.experts, count)
    expert = lax.broadcasted_iota(jnp.int32, table, 0)
    named, gates = jnp.zeros(table, F32), jnp.zeros(table, F32)
    for k in range(id_ref.shape[0]):
        here = jnp.broadcast_to(id_ref[k : k + 1, :], table) == expert
        named = jnp.where(here, 1.0, named)
        gates = jnp.where(here, jnp.broadcast_to(gate_ref[k : k + 1, :], table), gates)
    order = [lax.broadcasted_iota(jnp.int32, (count, count), n) for n in range(2)]
    earlier = jnp.where(order[0] < order[1], 1.0, 0.0).astype(BF16)
    ranks = named * (1.0 + jnp.dot(named.astype(BF16), earlier, preferred_element_type=F32))
    high = gates.astype(BF16)
    middle = (gates - high.astype(F32)).astype(BF16)
    low = (gates - high.astype(F32) - middle.astype(F32)).astype(BF16)
    for n, part in enumerate((ranks.astype(BF16), high, middle, low)):
        wide = jnp.dot(part, spread_ref[...], preferred_element_type=F32)
        tab_ref[n] = wide.reshape(tab_ref.shape[1:])

    blocks = og_ref.shape[1] // LANES
    tok_ref[...] = jnp.zeros_like(tok_ref)
    end_ref[...] = jnp.zeros_like(end_ref)
    for b in range(blocks):
        tok_ref[b * count : (b + 1) * count] = og_ref[:, b * LANES : (b + 1) * LANES]
    ends = og_ref[:, blocks * LANES :].astype(F32)
    end_ref[:, : ends.shape[1]] = ends
    ends = end_ref[...]
    tok_ref[blocks * count : (blocks + 1) * count] = ends.astype(BF16)
    ends = pltpu.roll(ends, LANES // 2, 1)
    tok_ref[(blocks + 1) * count : (blocks + 2) * count] = ends.astype(BF16)

    message = sbuf.shape[2:]
    width = wt_ref.shape[0]
    tokens, wants = tok_ref[...], wants_ref[...]

    def prepare(step, carry):
        x = (my_x + step) % z.nx
        shape = (z.slab,) + wants.shape
        hit = jnp.broadcast_to(tab_ref[0, x][:, None], shape) == wants[None]
        picked = 0.0
        for n in range(1, 4):
            part = jnp.where(hit, jnp.broadcast_to(tab_ref[n, x][:, None], shape), 0.0)
            part = part.reshape(-1, shape[2]).astype(BF16)
            picked = picked + jnp.dot(part, tokens, preferred_element_type=F32)
        sbuf[step] = picked.astype(BF16).reshape(sbuf.shape[1:])
        return carry

    lax.fori_loop(0, z.nx, prepare, 0)
    pl.semaphore_wait(barrier, z.experts + z.nz - 1)

    to_partner = send(hid_ref.at[1], theirs, th_s, th_r, expert=opposite)
    to_partner.start()

    def to_slab(n, carry):
        step = 1 + (n + z.nx // 2 - 1) % (z.nx - 1)
        x = (my_x + step) % z.nx

        def one(j, inner):
            send(
                sbuf.at[step, j], abuf.at[my_x, yc], dx_s.at[step], dx_r.at[step],
                expert=x * z.slab + j,
            ).start()
            return inner

        return lax.fori_loop(0, z.slab, one, carry)

    def to_own_slab(m, carry):
        j = (yc + m) % z.slab
        send(
            sbuf.at[0, j], abuf.at[my_x, yc], dx_s.at[0], dx_r.at[0], expert=my_x * z.slab + j
        ).start()
        return carry

    lax.fori_loop(0, z.nx - 1, to_slab, 0)
    lax.fori_loop(1, z.slab, to_own_slab, 0)
    abuf[my_x, yc] = sbuf[0, yc]

    lane = lax.broadcasted_iota(jnp.int32, rep_ref.shape, 1)
    has_second = jnp.sum(jnp.where(lane == ex, rep_ref[...], 0), axis=1, keepdims=True)
    row = lax.broadcasted_iota(jnp.int32, theirs.shape, 0)
    inside = jnp.where(row < z.half, row, row - z.half)
    second = jnp.broadcast_to(has_second, theirs.shape) == 1
    moved = jnp.where((inside < z.per_share // 2 * CAP) & second, 1.0, 0.0)
    to_partner.wait_recv()
    hbuf[dp] = (
        hid_ref[0].astype(F32) * (1.0 - moved) + theirs[...].astype(F32) * moved
    ).astype(BF16)
    to_z = [
        send(hbuf.at[dp], hbuf.at[dp], hz_s.at[k], hz_r.at[k], dp=at_z(k)) for k in range(1, z.nz)
    ]
    for copy in to_z:
        copy.start()
    to_other = [send(hbuf.at[dp], hbuf.at[dp], hy_s.at[0], hy_r.at[0], dp=other)]
    to_other[0].start()

    per_half = z.nx // 2
    came = abuf.at[my_x, pl.ds(0, z.slab - 1)]
    send(came, came, dx_s.at[0], dx_r.at[0], dp=other).wait_recv()
    for n in range(z.nx):
        slab = ((1 - y_lo) * per_half + n) % z.nx

        @pl.when(slab != my_x)
        def _():
            back = (my_x - slab + z.nx) % z.nx
            send(abuf.at[slab], abuf.at[slab], dx_s.at[back], dx_r.at[back], dp=other).wait_recv()

        arrived = abuf[slab].reshape(z.slab * message[0], message[1])
        taken = jnp.dot(take_ref[...], arrived, preferred_element_type=F32)
        taken = [taken[n * z.rows : (n + 1) * z.rows] for n in range(taken.shape[0] // z.rows)]
        ends = taken[-2] + pltpu.roll(taken[-1], LANES // 2, 1)
        dbuf[slab] = jnp.concatenate(taken[:-2] + [ends], axis=1).astype(BF16)
        part = jnp.dot(dbuf[slab][:, :width], wt_ref[...], preferred_element_type=F32)
        for h in range(2):
            pbuf[slab, h] = stacked(part[h * z.half : (h + 1) * z.half]).astype(BF16)
        if n < per_half:
            send(pbuf.at[slab], prec.at[n], py_s.at[n], py_r.at[n], dp=other).start()

    for q in range(per_half):
        send(pbuf.at[q], prec.at[q], py_s.at[q], py_r.at[q], dp=other).wait_recv()
        for h in range(2):
            both = pbuf[y_lo * per_half + q, h].astype(F32) + prec[q, h].astype(F32)
            to = 2 * q + h
            ssend[to] = both.astype(BF16)

            @pl.when(to != my_z)
            def _():
                k = (to - my_z + z.nz) % z.nz
                send(
                    ssend.at[to], zrec.at[my_z], rz_s.at[k], rz_r.at[k], dp=y_lo * z.nz + to
                ).start()

    for k in range(1, z.nz):
        to_z[k - 1].wait_recv()
        slot = at_z(z.nz - k)
        copy = send(hbuf.at[slot], hbuf.at[slot], hy_s.at[k], hy_r.at[k], dp=other)
        copy.start()
        to_other.append(copy)

    total = ssend[my_z].astype(F32)
    for k in range(1, z.nz):
        back = z.nz - k
        send(ssend.at[0], zrec.at[0], rz_s.at[k], rz_r.at[k], dp=at_z(k)).wait_recv()
        total = total + zrec[(my_z + back) % z.nz].astype(F32)
    few = fsend.shape[0] // 2
    going = total * moved
    fsend[...] = jnp.concatenate([going[:few], going[z.half : z.half + few]], axis=0).astype(BF16)
    last = send(fsend, frec, fx_s, fx_r, expert=opposite)
    last.start()
    hg_ref[0] = total - going

    for copy in to_other:
        copy.wait_recv()
    for slab in range(z.nx):
        pair = [hbuf[2 * slab + h].astype(F32) for h in range(2)]
        for side in range(2):
            piece = jnp.concatenate([p[side * z.half : (side + 1) * z.half] for p in pair], axis=0)
            hall[slab, :, side * piece.shape[1] : (side + 1) * piece.shape[1]] = piece.astype(BF16)
    rows_all = dbuf[...].reshape(z.nx * z.rows, dbuf.shape[2])
    tile = min(256, gd_ref.shape[1])

    def columns(n, carry):
        at = pl.ds(pl.multiple_of(n * tile, tile), tile)
        kept = hall[:, :, at].reshape(z.nx * z.rows, tile)
        full = lax.dot_general(
            rows_all, kept, (((0,), (0,)), ((), ())), preferred_element_type=F32
        )
        gd_ref[:, at] = full[:width].astype(BF16)
        return carry

    lax.fori_loop(0, gd_ref.shape[1] // tile, columns, 0)

    last.wait_recv()
    came = frec[...].astype(F32)
    empty = jnp.zeros((z.half - few, came.shape[1]), F32)
    hg_ref[1] = jnp.concatenate([came[:few], empty, came[few:], empty], axis=0)

    for copy in [to_partner] + to_z + to_other + [last]:
        copy.wait_send()
    for step in range(z.nx):
        sent = sbuf.at[step] if step else sbuf.at[0, pl.ds(0, z.slab - 1)]
        send(sent, sent, dx_s.at[step], dx_r.at[step], dp=other).wait_send()
    for q in range(per_half):
        send(pbuf.at[q], prec.at[q], py_s.at[q], py_r.at[q], dp=other).wait_send()
    for k in range(1, z.nz):
        send(ssend.at[0], zrec.at[0], rz_s.at[k], rz_r.at[k], dp=at_z(k)).wait_send()


def hidden_of(stored):
    width = stored.shape[-1] // 2
    gate_part = stored[..., :width].astype(F32)
    up_part = stored[..., width:].astype(F32)
    return (gate_part * jax.nn.sigmoid(gate_part) * up_part).astype(BF16)


def swiglu_back(hidden_grad, stored):
    width = stored.shape[-1] // 2
    gate_part = stored[..., :width].astype(F32)
    up_part = stored[..., width:].astype(F32)
    sigmoid_v = jax.nn.sigmoid(gate_part)
    gate_grad = hidden_grad * up_part * sigmoid_v * (1.0 + gate_part * (1.0 - sigmoid_v))
    up_grad = hidden_grad * gate_part * sigmoid_v
    return jnp.concatenate([gate_grad, up_grad], axis=-1).astype(BF16)


def on_device(z, out_grad, gate_weight, expert_ids, replicated, down_weight, pre_act):
    tokens, width = out_grad.shape
    hidden_width = pre_act.shape[3] // 2
    half_lanes = hidden_width // 2

    wants = packed_wants(tokens, width)
    blocks, message_rows = packing(width)
    spread = np.zeros((tokens, wants.shape[1]), np.float32)
    for b in range(blocks + 2):
        spread[:, b * tokens : (b + 1) * tokens] = np.eye(tokens)

    hidden = hidden_of(pre_act[0]).reshape(2, z.per_share, CAP, hidden_width)
    hidden = jnp.concatenate([hidden[:, n] for n in share_order(z)], axis=1)
    hidden = jnp.pad(hidden, ((0, 0), (0, z.half - z.share_rows), (0, 0)))
    hidden = hidden.reshape(2, z.half, 2, half_lanes).swapaxes(1, 2).reshape(2, z.rows, half_lanes)
    odd_rows = z.per_share // 2 * CAP
    weight = jnp.swapaxes(down_weight[0], 0, 1)
    take = jnp.asarray(unpacking(z, width), BF16)
    few = (2 * up_to(odd_rows, 8), half_lanes)

    chunk = (z.rows, half_lanes)
    dma = pltpu.SemaphoreType.DMA
    gd, hg = pl.pallas_call(
        functools.partial(kernel, z),
        out_shape=(
            jax.ShapeDtypeStruct((width, hidden_width), BF16),
            jax.ShapeDtypeStruct((2,) + chunk, F32),
        ),
        in_specs=[pl.BlockSpec(memory_space=pltpu.VMEM)] * 9,
        out_specs=(pl.BlockSpec(memory_space=pltpu.VMEM),) * 2,
        scratch_shapes=[
            pltpu.VMEM((wants.shape[1], LANES), BF16),
            pltpu.VMEM((tokens, LANES), F32),
            pltpu.VMEM((4, z.nx, z.slab, wants.shape[1]), F32),
            pltpu.VMEM((z.nx, z.slab, message_rows, LANES), BF16),
            pltpu.VMEM((z.nx, z.slab, message_rows, LANES), BF16),
            pltpu.VMEM(chunk, BF16),
            pltpu.VMEM((z.dp,) + chunk, BF16),
            pltpu.VMEM((z.nx, z.rows, hidden_width), BF16),
            pltpu.VMEM((z.nx, z.rows, up_to(width, LANES)), BF16),
            pltpu.VMEM((z.nx, 2) + chunk, BF16),
            pltpu.VMEM((z.nx // 2, 2) + chunk, BF16),
            pltpu.VMEM((z.nz,) + chunk, BF16),
            pltpu.VMEM((z.nz,) + chunk, BF16),
            pltpu.VMEM(few, BF16),
            pltpu.VMEM(few, BF16),
            dma, dma,
            dma((z.nz,)), dma((z.nz,)), dma((z.nz,)), dma((z.nz,)),
            dma((z.nx,)), dma((z.nx,)), dma((z.nx // 2,)), dma((z.nx // 2,)),
            dma((z.nz,)), dma((z.nz,)), dma, dma,
        ],
        compiler_params=pltpu.CompilerParams(
            collective_id=0, has_side_effects=True, vmem_limit_bytes=40 << 20
        ),
    )(
        out_grad, jnp.swapaxes(expert_ids, 0, 1), jnp.swapaxes(gate_weight, 0, 1), replicated[None],
        hidden, jnp.asarray(wants), jnp.asarray(spread, BF16), take, weight,
    )

    hg = hg.reshape(2, 2, z.half, half_lanes)[:, :, : z.share_rows]
    hg = hg.reshape(2, 2, z.per_share, CAP, half_lanes)
    placed = share_order(z)
    hg = jnp.concatenate([hg[:, :, placed.index(n)] for n in range(z.per_share)], axis=2)
    hg = hg.swapaxes(1, 2).reshape(2, z.share_rows, hidden_width)
    return (jnp.swapaxes(gd, 0, 1)[None], swiglu_back(hg, pre_act[0])[None])


def solution(mesh):
    in_specs = (
        P("expert", "dp"),
        P("expert", None),
        P("expert", None),
        P(),
        P("expert", None, "dp"),
        P("expert", None, "dp", None),
    )
    out_specs = (P("expert", None, "dp"), P("expert", None, "dp", None))
    return jax.shard_map(
        functools.partial(on_device, Sizes(mesh)),
        mesh=mesh, in_specs=in_specs, out_specs=out_specs, check_vma=False,
    )
```
